32 devices in a mesh: section: 2 (over core), region: 16 (over z, y, x).
Axes of the slice: x: 2, y: 2, z: 4, core: 2. Of those that a mesh axis runs over, the one named last changes fastest.
Arguments:
- hits: bfloat16 [2, 4096, 512], P('section', 'region'), may hold values from -6 to 6
- order: int32 [2, 16, 256], P(None, 'region'), may hold values from 0 to 255, each once within a row
- links: int32 [2, 32, 3], P(None, 'region'), may hold values from 0 to 31, as said below
- counts: int32 [2, 16], replicated, may hold values from 64 to 256, as said below
- w_qkv: bfloat16 [2, 512, 1536], P('section')
- w_out: bfloat16 [2, 512, 512], P('section'), may hold values from -0.25 to 0.25
- w_up: bfloat16 [2, 512, 2048], P('section'), may hold values from -0.25 to 0.25
- w_down: bfloat16 [2, 2048, 512], P('section'), may hold values from -0.125 to 0.125
Outputs:
- encoded: bfloat16 [2, 4096, 512], P('section', 'region')
The draws below stay inside these ranges and needn't reach their ends.
Inputs may be any that keep to these rules, and one draw needn't show every extreme that they name: `links`: entry 0 of patch g is g itself; the other entries are distinct patches other than g, at most 2 patches away from g along the curve. `counts`: in every event some region is full and some region holds 64 hits. `order`: each region's entries along the last dimension list each of its 256 hits once.
All inputs are finite; a program needn't handle non-finite values.
Results may differ from the reference program's by a relative error of at most 0.015.
Values may be sent and summed in bfloat16 or wider, within the bound.
A program may use at most 64 MiB of HBM per device.

```python
import jax
import jax.numpy as jnp
from jax import lax

D = 512
HEADS = 8
FF = 2048
HEAD_DIM = 64
PATCH = 128
REACH = 2
LINKS = 3
H_DEV = 256
BLOCKS = 2
MICRO = 2
REGIONS = 16
HITS = 4096
TOTAL_PATCHES = 32


def draw_links(key, part):
    slots = jnp.arange(2 * REACH)
    offsets = slots - REACH + (slots >= REACH).astype(jnp.int32)
    patches_all = jnp.arange(TOTAL_PATCHES)
    target = patches_all[None, :, None] + offsets[None, None, :]
    target = jnp.broadcast_to(target, (MICRO, TOTAL_PATCHES, 2 * REACH))
    raw = jax.random.randint(key, (MICRO, TOTAL_PATCHES, 2 * REACH), 0, 1 << 20)
    score = raw * (2 * REACH) + slots[None, None, :]
    inside = (target >= 0) & (target < TOTAL_PATCHES)
    score = jnp.where(inside, score, score - (1 << 24))
    chosen_score, picked = lax.top_k(score, LINKS - 1)
    chosen = jnp.take_along_axis(target, picked, axis=2)
    itself = jnp.broadcast_to(patches_all[None, :, None], (MICRO, TOTAL_PATCHES, 1))
    return jnp.concatenate([itself, chosen], axis=2).astype(jnp.int32)


def draw_counts(key, part):
    first_key, second_key, third_key = jax.random.split(key, 3)
    base = jax.random.randint(first_key, (MICRO, REGIONS), H_DEV // 4, H_DEV + 1)
    full_region = jax.random.randint(second_key, (MICRO, 1), 0, REGIONS)
    low_region = (full_region + 1 + jax.random.randint(third_key, (MICRO, 1), 0, REGIONS - 1)) % REGIONS
    region_ids = jnp.arange(REGIONS)[None, :]
    base = jnp.where(region_ids == full_region, H_DEV, jnp.where(region_ids == low_region, H_DEV // 4, base))
    return base.astype(jnp.int32)


def draw_w_qkv(key, part):
    first_key = jax.random.fold_in(key, 0)
    values = jax.random.normal(first_key, (BLOCKS, D, 3 * D), jnp.float32) * D ** (-0.5)
    return values.astype(jnp.bfloat16)


def shard_levels(key, extent, pieces, low, top_value):
    def one(dim, blocks):
        heights = jax.random.uniform(jax.random.fold_in(jax.random.fold_in(key, 6), dim), (blocks,), jnp.float32, low / len(pieces), top_value / len(pieces))
        return jnp.repeat(jnp.exp(heights), extent[dim] // blocks).reshape((-1,) + (1,) * (len(extent) - dim - 1))

    gain = one(*pieces[0])
    for cut in pieces[1:]:
        gain = gain * one(*cut)
    return gain


def gaussian(key, dims, width, bound, cuts=(), held_as=jnp.bfloat16):
    entries = width * jax.random.normal(key, dims, jnp.float32)
    if cuts:
        entries = entries * shard_levels(key, dims, cuts, -0.22, 0.18)
    return jnp.clip(entries, -bound, bound).astype(held_as)


def setup_inputs(seed: int = 0) -> dict:
    arg_keys = jax.random.split(jax.random.key(seed), 9)
    hits = gaussian(arg_keys[0], (MICRO, HITS, D), 1.0, 6.0, ((0, 2), (1, 16)))
    order = jax.vmap(lambda own: jax.random.permutation(own, H_DEV))(jax.random.split(arg_keys[1], MICRO * REGIONS)).reshape((MICRO, REGIONS, H_DEV)).astype(jnp.int32)
    links = draw_links(jax.random.fold_in(arg_keys[8], 71), 0)
    counts = draw_counts(jax.random.fold_in(arg_keys[8], 71), 0)
    w_qkv = draw_w_qkv(jax.random.fold_in(arg_keys[8], 71), 0)
    w_out = gaussian(arg_keys[5], (BLOCKS, D, D), D ** -0.5, 0.25, ((0, 2),))
    w_up = gaussian(arg_keys[6], (BLOCKS, D, FF), D ** -0.5, 0.25, ((0, 2),))
    w_down = gaussian(arg_keys[7], (BLOCKS, FF, D), FF ** -0.5, 0.125, ((0, 2),))
    return {"hits": hits, "order": order, "links": links, "counts": counts, "w_qkv": w_qkv, "w_out": w_out, "w_up": w_up, "w_down": w_down}


epsilon = 1e-05

def normalize(state):
    values = state.astype(jnp.float32)
    center = lax.optimization_barrier(jnp.mean(values, axis=-1, keepdims=True))
    spread = lax.optimization_barrier(jnp.mean((values - center) ** 2, axis=-1, keepdims=True))
    return ((values - center) * lax.rsqrt(spread + epsilon)).astype(jnp.bfloat16)

def attend(queries, padded_keys, padded_values, padded_valid, index):
    patch_count = index.shape[0]
    links_count = index.shape[1]
    query_part = queries.reshape(patch_count, PATCH, HEADS, HEAD_DIM).astype(jnp.float32)
    key_part = padded_keys.reshape(-1, PATCH, HEADS, HEAD_DIM)[index]
    key_part = key_part.reshape(patch_count, links_count * PATCH, HEADS, HEAD_DIM).astype(jnp.float32)
    value_part = padded_values.reshape(-1, PATCH, HEADS, HEAD_DIM)[index]
    value_part = value_part.reshape(patch_count, links_count * PATCH, HEADS, HEAD_DIM).astype(jnp.float32)
    key_mask = padded_valid.reshape(-1, PATCH)[index].reshape(patch_count, links_count * PATCH)
    scores = jnp.einsum('pqhd,pkhd->phqk', query_part, key_part) * HEAD_DIM ** (-0.5)
    scores = jnp.where(key_mask[:, None, None, :], scores, -1e+30)
    highest = lax.optimization_barrier(jnp.max(scores, axis=-1, keepdims=True))
    weights = jnp.exp(scores - highest)
    probs = (weights / lax.optimization_barrier(jnp.sum(weights, axis=-1, keepdims=True))).astype(jnp.bfloat16)
    output = jnp.einsum('phqk,pkhd->pqhd', probs.astype(jnp.float32), value_part)
    return output.reshape(patch_count * PATCH, D).astype(jnp.bfloat16)

def run_block(state, index, padded_valid, weight_qkv, weight_out, weight_up, weight_down):
    normed = normalize(state)
    mixed = jnp.dot(normed, weight_qkv, preferred_element_type=jnp.float32).astype(jnp.bfloat16)
    queries = mixed[:, :D]
    margin = REACH * PATCH
    padded_keys = jnp.pad(mixed[:, D:2 * D], ((margin, margin), (0, 0)))
    padded_values = jnp.pad(mixed[:, 2 * D:], ((margin, margin), (0, 0)))
    attended = attend(queries, padded_keys, padded_values, padded_valid, index)
    middle = (state.astype(jnp.float32) + jnp.dot(attended, weight_out, preferred_element_type=jnp.float32)).astype(jnp.bfloat16)
    normed_mlp = normalize(middle)
    hidden = jax.nn.gelu(jnp.dot(normed_mlp, weight_up, preferred_element_type=jnp.float32), approximate=False).astype(jnp.bfloat16)
    return (middle.astype(jnp.float32) + jnp.dot(hidden, weight_down, preferred_element_type=jnp.float32)).astype(jnp.bfloat16)

def reference(hits, order, links, counts, w_qkv, w_out, w_up, w_down):

    def one_event(event_index):
        regional = hits[event_index].reshape(REGIONS, H_DEV, D)
        ordered = regional[jnp.arange(REGIONS)[:, None], order[event_index]].reshape(HITS, D)
        position = jnp.arange(HITS)
        valid = position % H_DEV < counts[event_index][position // H_DEV]
        margin = REACH * PATCH
        padded_valid = jnp.pad(valid, (margin, margin))
        index = (links[event_index] + REACH).astype(jnp.int32)
        state = ordered
        for block_index in range(BLOCKS):
            state = run_block(state, index, padded_valid, w_qkv[block_index], w_out[block_index], w_up[block_index], w_down[block_index])
        return jnp.where(valid[:, None], state, jnp.zeros_like(state))
    return lax.map(one_event, jnp.arange(MICRO))
```

```python
import functools

import jax
import jax.numpy as jnp
from jax import lax
from jax.experimental import pallas as pl
from jax.experimental.pallas import tpu as pltpu
from jax.sharding import PartitionSpec as P

HEADS = 8
REACH = 2
FF_PARTS = 4
LANES = 128
epsilon = 1e-05
MESH = pl.DeviceIdType.MESH


def product(left, right):
    return jnp.dot(left, right, preferred_element_type=jnp.float32)


def normalize(values):
    center = jnp.mean(values, axis=-1, keepdims=True)
    moved = values - center
    spread = jnp.mean(moved * moved, axis=-1, keepdims=True)
    return (moved * lax.rsqrt(spread + epsilon)).astype(jnp.bfloat16)


def gelu(values):
    return 0.5 * values * (1.0 + lax.erf(values * (0.5**0.5)))


def kernel(
    segments,
    regions,
    links_ref,
    counts_ref,
    hits_ref,
    order_ref,
    wqkv_hbm,
    wout_hbm,
    wup_hbm,
    wdown_hbm,
    out_ref,
    wqkv,
    wout,
    wup,
    wdown,
    state,
    normed,
    queries,
    keys,
    values,
    attended,
    weight_sems,
    weight_send_sems,
    halo_sems,
    halo_send_sems,
):
    section = lax.axis_index("section")
    region = lax.axis_index("region")
    rows, width = state.shape
    patches = links_ref.shape[1]
    links_count = links_ref.shape[2]
    patch_rows = rows // patches
    margin = REACH * patch_rows
    head_width = width // HEADS
    group = LANES // head_width
    ff_part = wup.shape[2] // FF_PARTS
    has_left = region > 0
    has_right = region < regions - 1
    others = [lax.rem(section + i, segments) for i in range(1, segments)]

    barrier = pltpu.get_barrier_semaphore()
    for other in others:
        pl.semaphore_signal(barrier, inc=1, device_id={"section": other}, device_id_type=MESH)

    @pl.when(has_left)
    def _():
        pl.semaphore_signal(barrier, inc=1, device_id={"region": region - 1}, device_id_type=MESH)

    @pl.when(has_right)
    def _():
        pl.semaphore_signal(barrier, inc=1, device_id={"region": region + 1}, device_id_type=MESH)

    def weight_pieces(block):
        pieces = [(wqkv_hbm.at[0], wqkv.at[block]), (wout_hbm.at[0], wout.at[block])]
        for part in range(FF_PARTS):
            span = pl.ds(part * ff_part, ff_part)
            pieces.append((wup_hbm.at[0, :, span], wup.at[block, :, span]))
            pieces.append((wdown_hbm.at[0, span, :], wdown.at[block, span, :]))
        return pieces

    own_pieces = weight_pieces(section)
    piece_count = len(own_pieces)
    for i, (source, target) in enumerate(own_pieces):
        pltpu.make_async_copy(source, target, weight_sems.at[section, i]).start()

    peers = segments - 1 + (region > 0).astype(jnp.int32) + (region < regions - 1).astype(jnp.int32)
    pl.semaphore_wait(barrier, peers)

    def weight_sends():
        sends = []
        for n, other in enumerate(others):
            for i, (source, target) in enumerate(own_pieces):
                sends.append(
                    pltpu.make_async_remote_copy(
                        src_ref=source,
                        dst_ref=target,
                        send_sem=weight_send_sems.at[n, i],
                        recv_sem=weight_sems.at[section, i],
                        device_id={"section": other},
                        device_id_type=MESH,
                    )
                )
        return sends

    for send in weight_sends():
        send.start()

    def wait_weight(block, i):
        target = weight_pieces(block)[i][1]
        pltpu.make_async_copy(target, target, weight_sems.at[block, i]).wait()

    def halo_send(block, way):
        source = margin if way == 0 else rows
        target = margin + rows if way == 0 else 0
        return pltpu.make_async_remote_copy(
            src_ref=normed.at[block, pl.ds(source, margin)],
            dst_ref=normed.at[block, pl.ds(target, margin)],
            send_sem=halo_send_sems.at[block, way],
            recv_sem=halo_sems.at[block, way],
            device_id={"region": region - 1 if way == 0 else region + 1},
            device_id_type=MESH,
        )

    slots = lax.broadcasted_iota(jnp.int32, (rows, rows), 0)
    picks = (slots == order_ref[section]).astype(jnp.float32).astype(jnp.bfloat16)
    state[...] = lax.dot_general(
        picks, hits_ref[0], (((0,), (0,)), ((), ())), preferred_element_type=jnp.float32
    )
    lane = lax.broadcasted_iota(jnp.int32, (1, LANES), 1)
    head_lanes = [lane // head_width == j for j in range(group)]
    key_slot = lax.broadcasted_iota(jnp.int32, (1, patch_rows), 1)
    ones = jnp.ones((links_count * patch_rows, LANES), jnp.bfloat16)

    def near_pair(block, start, count):
        both = product(
            normed[block, pl.ds(start, count), :], wqkv[block, :, pl.ds(width, 2 * width)]
        ).astype(jnp.bfloat16)
        first = start // patch_rows
        for i in range(count // patch_rows):
            piece = both[i * patch_rows : (i + 1) * patch_rows]
            keys[first + i] = piece[:, :width]
            values[first + i] = piece[:, width:]

    def run_block(block, carry):
        normed[block, pl.ds(margin, rows), :] = normalize(state[...])

        @pl.when(has_left)
        def _():
            halo_send(block, 0).start()

        @pl.when(has_right)
        def _():
            halo_send(block, 1).start()

        wait_weight(block, 0)
        queries[...] = (
            product(normed[block, pl.ds(margin, rows), :], wqkv[block, :, pl.ds(0, width)])
            .astype(jnp.bfloat16)
            * head_width ** (-0.5)
        ).astype(jnp.bfloat16)
        near_pair(block, margin, rows)

        @pl.when(has_left)
        def _():
            halo_send(block, 1).wait_recv()

        @pl.when(has_right)
        def _():
            halo_send(block, 0).wait_recv()

        @pl.when(jnp.logical_not(has_left))
        def _():
            normed[block, pl.ds(0, margin), :] = jnp.zeros((margin, width), jnp.bfloat16)

        @pl.when(jnp.logical_not(has_right))
        def _():
            normed[block, pl.ds(margin + rows, margin), :] = jnp.zeros((margin, width), jnp.bfloat16)

        near_pair(block, 0, margin)
        near_pair(block, margin + rows, margin)

        for patch in range(patches):
            linked = [links_ref[section, patch, j] for j in range(links_count)]
            near = [
                jnp.clip(link - region * patches + REACH, 0, keys.shape[0] - 1) for link in linked
            ]
            mask = jnp.concatenate(
                [
                    key_slot < counts_ref[section, link // patches] - lax.rem(link, patches) * patch_rows
                    for link in linked
                ],
                axis=1,
            )
            span = pl.ds(patch * patch_rows, patch_rows)
            for first in range(0, width, LANES):
                columns = pl.ds(first, LANES)
                own = queries[span, columns]
                stacked = jnp.concatenate(
                    [jnp.where(chosen, own, jnp.zeros_like(own)) for chosen in head_lanes], axis=0
                )
                near_keys = jnp.concatenate([keys[i, :, columns] for i in near], axis=0)
                near_values = jnp.concatenate([values[i, :, columns] for i in near], axis=0)
                scores = lax.dot_general(
                    stacked, near_keys, (((1,), (1,)), ((), ())), preferred_element_type=jnp.float32
                )
                scores = jnp.where(mask, scores, -1e30)
                weights = jnp.exp(scores - jnp.max(scores, axis=-1, keepdims=True)).astype(jnp.bfloat16)
                mixed = product(weights, jnp.concatenate([near_values, ones], axis=1))
                mixed = mixed[:, :LANES] / mixed[:, LANES:]
                result = mixed[:patch_rows]
                for j in range(1, group):
                    result = jnp.where(
                        head_lanes[j], mixed[j * patch_rows : (j + 1) * patch_rows], result
                    )
                attended[span, columns] = result.astype(jnp.bfloat16)

        wait_weight(block, 1)
        middle = (state[...] + product(attended[...], wout[block])).astype(jnp.bfloat16)
        middle = middle.astype(jnp.float32)
        normed_mlp = normalize(middle)
        total = middle
        for part in range(FF_PARTS):
            span = pl.ds(part * ff_part, ff_part)
            wait_weight(block, 2 + 2 * part)
            hidden = gelu(product(normed_mlp, wup[block, :, span])).astype(jnp.bfloat16)
            wait_weight(block, 3 + 2 * part)
            total = total + product(hidden, wdown[block, span, :])
        state[...] = total.astype(jnp.bfloat16).astype(jnp.float32)

        @pl.when(has_left)
        def _():
            halo_send(block, 0).wait_send()

        @pl.when(has_right)
        def _():
            halo_send(block, 1).wait_send()

        return carry

    lax.fori_loop(0, segments, run_block, 0)
    out_ref[0] = state[...].astype(jnp.bfloat16)
    for send in weight_sends():
        send.wait_send()


def per_device(hits, order, links, counts, w_qkv, w_out, w_up, w_down):
    segments = lax.axis_size("section")
    regions = lax.axis_size("region")
    rows, width = hits.shape[1:]
    hidden = w_up.shape[2]
    patches = links.shape[1]
    patch_rows = rows // patches
    margin = REACH * patch_rows
    near_rows = rows + 2 * margin
    assert margin <= rows and w_qkv.shape[0] == 1
    piece_count = 2 + 2 * FF_PARTS
    vmem = pl.BlockSpec(memory_space=pltpu.VMEM)
    smem = pl.BlockSpec(memory_space=pltpu.SMEM)
    hbm = pl.BlockSpec(memory_space=pl.ANY)
    bf16 = jnp.bfloat16
    encoded = pl.pallas_call(
        functools.partial(kernel, segments, regions),
        out_shape=jax.ShapeDtypeStruct((1, rows, width), bf16),
        in_specs=[smem, smem, vmem, vmem, hbm, hbm, hbm, hbm],
        out_specs=vmem,
        scratch_shapes=[
            pltpu.VMEM((segments,) + w_qkv.shape[1:], bf16),
            pltpu.VMEM((segments,) + w_out.shape[1:], bf16),
            pltpu.VMEM((segments,) + w_up.shape[1:], bf16),
            pltpu.VMEM((segments,) + w_down.shape[1:], bf16),
            pltpu.VMEM((rows, width), jnp.float32),
            pltpu.VMEM((segments, near_rows, width), bf16),
            pltpu.VMEM((rows, width), bf16),
            pltpu.VMEM((near_rows // patch_rows, patch_rows, width), bf16),
            pltpu.VMEM((near_rows // patch_rows, patch_rows, width), bf16),
            pltpu.VMEM((rows, width), bf16),
            pltpu.SemaphoreType.DMA((segments, piece_count)),
            pltpu.SemaphoreType.DMA((segments - 1, piece_count)),
            pltpu.SemaphoreType.DMA((segments, 2)),
            pltpu.SemaphoreType.DMA((segments, 2)),
        ],
        compiler_params=pltpu.CompilerParams(
            collective_id=0, has_side_effects=True, vmem_limit_bytes=48 * 2**20
        ),
        name="blocks",
    )(links, counts, hits, order, w_qkv, w_out, w_up, w_down)
    own_count = counts[lax.axis_index("section"), lax.axis_index("region")]
    keep = jnp.arange(rows) < own_count
    return jnp.where(keep[None, :, None], encoded, jnp.zeros_like(encoded))


def solution(mesh):
    in_specs = (
        P("section", "region", None),
        P(None, "region", None),
        P(None, "region", None),
        P(),
        P("section", None, None),
        P("section", None, None),
        P("section", None, None),
        P("section", None, None),
    )
    out_specs = P("section", "region", None)
    return jax.shard_map(
        per_device, mesh=mesh, in_specs=in_specs, out_specs=out_specs, check_vma=False
    )
```

```python
import functools

import jax
import jax.numpy as jnp
from jax import lax
from jax.experimental import pallas as pl
from jax.experimental.pallas import tpu as pltpu
from jax.sharding import PartitionSpec as P

HEADS = 8
REACH = 2
FF_PARTS = 4
HALO_PARTS = 4
LANES = 128
epsilon = 1e-05
MESH = pl.DeviceIdType.MESH


def product(left, right):
    return jnp.dot(left, right, preferred_element_type=jnp.float32)


def normalize(values):
    center = jnp.mean(values, axis=-1, keepdims=True)
    moved = values - center
    spread = jnp.mean(moved * moved, axis=-1, keepdims=True)
    return (moved * lax.rsqrt(spread + epsilon)).astype(jnp.bfloat16)


def gelu(values):
    size = jnp.abs(values)
    t = pl.reciprocal(1.0 + (0.3275911 * 0.5**0.5) * size, approx=True)
    series = 1.061405429 * t - 1.453152027
    series = series * t + 1.421413741
    series = series * t - 0.284496736
    series = series * t + 0.254829592
    tail = (series * t) * jnp.exp(-0.5 * (values * values))
    return jnp.maximum(values, 0.0) - (0.5 * size) * tail


def kernel(
    segments,
    regions,
    links_ref,
    counts_ref,
    hits_ref,
    order_ref,
    wqkv_hbm,
    wout_hbm,
    wup_hbm,
    wdown_hbm,
    out_ref,
    wqkv,
    wout,
    wup,
    wdown,
    state,
    normed,
    queries,
    keys,
    values,
    attended,
    weight_sems,
    weight_send_sems,
    halo_sems,
    halo_send_sems,
):
    section = lax.axis_index("section")
    region = lax.axis_index("region")
    rows, width = state.shape
    patches = links_ref.shape[1]
    links_count = links_ref.shape[2]
    patch_rows = rows // patches
    chunk = rows // HALO_PARTS
    head_width = width // HEADS
    group = LANES // head_width
    ff_part = wup.shape[2] // FF_PARTS
    parity = lax.rem(region, 2)
    near_slot = 2 * (1 - parity)
    far_slot = 2 * parity
    buddy = region + 1 - 2 * parity
    far_target = region + 2 - 4 * parity
    far_source = region - 2 + 4 * parity
    has_target = jnp.logical_and(far_target >= 0, far_target < regions)
    has_source = jnp.logical_and(far_source >= 0, far_source < regions)
    others = [lax.rem(section + i, segments) for i in range(1, segments)]

    barrier = pltpu.get_barrier_semaphore()
    for other in others:
        pl.semaphore_signal(barrier, inc=1, device_id={"section": other}, device_id_type=MESH)

    pl.semaphore_signal(barrier, inc=1, device_id={"region": buddy}, device_id_type=MESH)

    @pl.when(has_source)
    def _():
        pl.semaphore_signal(barrier, inc=1, device_id={"region": far_source}, device_id_type=MESH)

    def weight_pieces(block):
        pieces = [(wqkv_hbm.at[0], wqkv.at[block]), (wout_hbm.at[0], wout.at[block])]
        for part in range(FF_PARTS):
            span = pl.ds(part * ff_part, ff_part)
            pieces.append((wup_hbm.at[0, :, span], wup.at[block, :, span]))
            pieces.append((wdown_hbm.at[0, span, :], wdown.at[block, span, :]))
        return pieces

    own_pieces = weight_pieces(section)
    piece_count = len(own_pieces)
    for i, (source, target) in enumerate(own_pieces):
        pltpu.make_async_copy(source, target, weight_sems.at[section, i]).start()

    peers = segments + has_target.astype(jnp.int32)
    pl.semaphore_wait(barrier, peers)

    def weight_sends():
        sends = []
        for n, other in enumerate(others):
            for i, (source, target) in enumerate(own_pieces):
                sends.append(
                    pltpu.make_async_remote_copy(
                        src_ref=source,
                        dst_ref=target,
                        send_sem=weight_send_sems.at[n, i],
                        recv_sem=weight_sems.at[section, i],
                        device_id={"section": other},
                        device_id_type=MESH,
                    )
                )
        return sends

    for send in weight_sends():
        send.start()

    def wait_weight(block, i):
        target = weight_pieces(block)[i][1]
        pltpu.make_async_copy(target, target, weight_sems.at[block, i]).wait()

    def halo_send(block, way, part):
        span = pl.ds(part * chunk, chunk)
        return pltpu.make_async_remote_copy(
            src_ref=normed.at[block, 1 if way == 0 else near_slot, span],
            dst_ref=normed.at[block, far_slot, span],
            send_sem=halo_send_sems.at[block, way, part],
            recv_sem=halo_sems.at[block, way, part],
            device_id={"region": buddy if way == 0 else far_target},
            device_id_type=MESH,
        )

    slots = lax.broadcasted_iota(jnp.int32, (rows, rows), 0)
    picks = (slots == order_ref[section]).astype(jnp.float32).astype(jnp.bfloat16)
    state[...] = lax.dot_general(
        picks, hits_ref[0], (((0,), (0,)), ((), ())), preferred_element_type=jnp.float32
    )
    lane = lax.broadcasted_iota(jnp.int32, (1, LANES), 1)
    head_lanes = [lane // head_width == j for j in range(group)]
    key_slot = lax.broadcasted_iota(jnp.int32, (1, patch_rows), 1)
    ones = jnp.ones((links_count * patch_rows, LANES), jnp.bfloat16)

    def near_pair(block, slot):
        both = product(
            normed[block, slot], wqkv[block, :, pl.ds(width, 2 * width)]
        ).astype(jnp.bfloat16)
        for i in range(patches):
            piece = both[i * patch_rows : (i + 1) * patch_rows]
            keys[slot * patches + i] = piece[:, :width]
            values[slot * patches + i] = piece[:, width:]

    def run_block(block, carry):
        normed[block, 1] = normalize(state[...])
        for part in range(HALO_PARTS):
            halo_send(block, 0, part).start()

        wait_weight(block, 0)
        queries[...] = (
            product(normed[block, 1], wqkv[block, :, pl.ds(0, width)]).astype(jnp.bfloat16)
            * head_width ** (-0.5)
        ).astype(jnp.bfloat16)
        near_pair(block, 1)

        for part in range(HALO_PARTS):
            halo_send(block, 0, part).wait_recv()

            @pl.when(has_target)
            def _():
                halo_send(block, 1, part).start()

        near_pair(block, near_slot)

        @pl.when(has_source)
        def _():
            for part in range(HALO_PARTS):
                halo_send(block, 1, part).wait_recv()

        @pl.when(jnp.logical_not(has_source))
        def _():
            normed[block, far_slot] = jnp.zeros((rows, width), jnp.bfloat16)

        near_pair(block, far_slot)

        for patch in range(patches):
            linked = [links_ref[section, patch, j] for j in range(links_count)]
            near = [
                jnp.clip(link - region * patches + REACH, 0, keys.shape[0] - 1) for link in linked
            ]
            mask = jnp.concatenate(
                [
                    key_slot < counts_ref[section, link // patches] - lax.rem(link, patches) * patch_rows
                    for link in linked
                ],
                axis=1,
            )
            span = pl.ds(patch * patch_rows, patch_rows)
            for first in range(0, width, LANES):
                columns = pl.ds(first, LANES)
                own = queries[span, columns]
                stacked = jnp.concatenate(
                    [jnp.where(chosen, own, jnp.zeros_like(own)) for chosen in head_lanes], axis=0
                )
                near_keys = jnp.concatenate([keys[i, :, columns] for i in near], axis=0)
                near_values = jnp.concatenate([values[i, :, columns] for i in near], axis=0)
                scores = lax.dot_general(
                    stacked, near_keys, (((1,), (1,)), ((), ())), preferred_element_type=jnp.float32
                )
                scores = jnp.where(mask, scores, -1e30)
                weights = jnp.exp(scores - jnp.max(scores, axis=-1, keepdims=True)).astype(jnp.bfloat16)
                mixed = product(weights, jnp.concatenate([near_values, ones], axis=1))
                mixed = mixed[:, :LANES] / mixed[:, LANES:]
                result = mixed[:patch_rows]
                for j in range(1, group):
                    result = jnp.where(
                        head_lanes[j], mixed[j * patch_rows : (j + 1) * patch_rows], result
                    )
                attended[span, columns] = result.astype(jnp.bfloat16)

        wait_weight(block, 1)
        middle = (state[...] + product(attended[...], wout[block])).astype(jnp.bfloat16)
        middle = middle.astype(jnp.float32)
        normed_mlp = normalize(middle)
        total = middle
        for part in range(FF_PARTS):
            span = pl.ds(part * ff_part, ff_part)
            wait_weight(block, 2 + 2 * part)
            hidden = gelu(product(normed_mlp, wup[block, :, span])).astype(jnp.bfloat16)
            wait_weight(block, 3 + 2 * part)
            total = total + product(hidden, wdown[block, span, :])
        state[...] = total.astype(jnp.bfloat16).astype(jnp.float32)

        for part in range(HALO_PARTS):
            halo_send(block, 0, part).wait_send()

        @pl.when(has_target)
        def _():
            for part in range(HALO_PARTS):
                halo_send(block, 1, part).wait_send()

        return carry

    lax.fori_loop(0, segments, run_block, 0)
    row = lax.broadcasted_iota(jnp.int32, (rows, 1), 0)
    kept = jnp.where(row < counts_ref[section, region], state[...], 0.0)
    out_ref[0] = kept.astype(jnp.bfloat16)
    for send in weight_sends():
        send.wait_send()


def per_device(hits, order, links, counts, w_qkv, w_out, w_up, w_down):
    segments = lax.axis_size("section")
    regions = lax.axis_size("region")
    rows, width = hits.shape[1:]
    patches = links.shape[1]
    patch_rows = rows // patches
    near_patches = patches + 2 * REACH
    assert patches == REACH and regions % 2 == 0 and w_qkv.shape[0] == 1
    piece_count = 2 + 2 * FF_PARTS
    vmem = pl.BlockSpec(memory_space=pltpu.VMEM)
    smem = pl.BlockSpec(memory_space=pltpu.SMEM)
    hbm = pl.BlockSpec(memory_space=pltpu.HBM)
    bf16 = jnp.bfloat16
    return pl.pallas_call(
        functools.partial(kernel, segments, regions),
        out_shape=jax.ShapeDtypeStruct((1, rows, width), bf16),
        in_specs=[smem, smem, vmem, vmem, hbm, hbm, hbm, hbm],
        out_specs=vmem,
        scratch_shapes=[
            pltpu.VMEM((segments,) + w_qkv.shape[1:], bf16),
            pltpu.VMEM((segments,) + w_out.shape[1:], bf16),
            pltpu.VMEM((segments,) + w_up.shape[1:], bf16),
            pltpu.VMEM((segments,) + w_down.shape[1:], bf16),
            pltpu.VMEM((rows, width), jnp.float32),
            pltpu.VMEM((segments, 3, rows, width), bf16),
            pltpu.VMEM((rows, width), bf16),
            pltpu.VMEM((near_patches, patch_rows, width), bf16),
            pltpu.VMEM((near_patches, patch_rows, width), bf16),
            pltpu.VMEM((rows, width), bf16),
            pltpu.SemaphoreType.DMA((segments, piece_count)),
            pltpu.SemaphoreType.DMA((segments - 1, piece_count)),
            pltpu.SemaphoreType.DMA((segments, 2, HALO_PARTS)),
            pltpu.SemaphoreType.DMA((segments, 2, HALO_PARTS)),
        ],
        compiler_params=pltpu.CompilerParams(
            collective_id=0, has_side_effects=True, vmem_limit_bytes=60 * 2**20
        ),
        name="blocks",
    )(links, counts, hits, order, w_qkv, w_out, w_up, w_down)


def solution(mesh):
    in_specs = (
        P("section", "region", None),
        P(None, "region", None),
        P(None, "region", None),
        P(),
        P("section", None, None),
        P("section", None, None),
        P("section", None, None),
        P("section", None, None),
    )
    out_specs = P("section", "region", None)
    return jax.shard_map(
        per_device, mesh=mesh, in_specs=in_specs, out_specs=out_specs, check_vma=False
    )
```

```python
import functools
import math

import jax
import jax.numpy as jnp
from jax import lax
from jax.experimental import pallas as pl
from jax.experimental.pallas import tpu as pltpu
from jax.sharding import PartitionSpec as P

HEADS = 8
REACH = 2
FF_PARTS = 4
HALO_PARTS = 4
LANES = 128
epsilon = 1e-05
MESH = pl.DeviceIdType.MESH


def product(left, right):
    return jnp.dot(left, right, preferred_element_type=jnp.float32)


def normalize(values):
    center = jnp.mean(values, axis=-1, keepdims=True)
    moved = values - center
    spread = jnp.mean(moved * moved, axis=-1, keepdims=True)
    return (moved * lax.rsqrt(spread + epsilon)).astype(jnp.bfloat16)


def gelu(values):
    size = jnp.abs(values)
    t = pl.reciprocal(1.0 + (0.3275911 * 0.5**0.5) * size, approx=True)
    series = 1.061405429 * t - 1.453152027
    series = series * t + 1.421413741
    series = series * t - 0.284496736
    series = series * t + 0.254829592
    tail = (series * t) * jnp.exp(-0.5 * (values * values))
    return jnp.maximum(values, 0.0) - (0.5 * size) * tail


def kernel(
    segments,
    regions,
    links_hbm,
    counts_hbm,
    hits_hbm,
    order_hbm,
    wqkv_hbm,
    wout_hbm,
    wup_hbm,
    wdown_hbm,
    out_ref,
    wqkv,
    wout,
    wup,
    wdown,
    state,
    normed,
    queries,
    keys,
    values,
    attended,
    hits_ref,
    order_ref,
    links_ref,
    counts_ref,
    input_sems,
    weight_sems,
    weight_send_sems,
    halo_sems,
    halo_send_sems,
):
    section = lax.axis_index("section")
    region = lax.axis_index("region")
    rows, width = state.shape
    patches = links_ref.shape[1]
    links_count = links_ref.shape[2]
    patch_rows = rows // patches
    chunk = rows // HALO_PARTS
    head_width = width // HEADS
    group = LANES // head_width
    ff_part = wup.shape[2] // FF_PARTS
    parity = lax.rem(region, 2)
    near_slot = 2 * (1 - parity)
    far_slot = 2 * parity
    buddy = region + 1 - 2 * parity
    far_target = region + 2 - 4 * parity
    far_source = region - 2 + 4 * parity
    has_target = jnp.logical_and(far_target >= 0, far_target < regions)
    has_source = jnp.logical_and(far_source >= 0, far_source < regions)
    others = [lax.rem(section + i, segments) for i in range(1, segments)]

    hits_copy = pltpu.make_async_copy(hits_hbm.at[0], hits_ref, input_sems.at[0])
    order_copy = pltpu.make_async_copy(order_hbm.at[section], order_ref, input_sems.at[1])
    links_copy = pltpu.make_async_copy(links_hbm, links_ref, input_sems.at[2])
    counts_copy = pltpu.make_async_copy(counts_hbm, counts_ref, input_sems.at[3])
    hits_copy.start()
    order_copy.start()
    links_copy.start()
    counts_copy.start()
    barrier = pltpu.get_barrier_semaphore()
    for other in others:
        pl.semaphore_signal(barrier, inc=1, device_id={"section": other}, device_id_type=MESH)

    pl.semaphore_signal(barrier, inc=1, device_id={"region": buddy}, device_id_type=MESH)

    @pl.when(has_source)
    def _():
        pl.semaphore_signal(barrier, inc=1, device_id={"region": far_source}, device_id_type=MESH)

    def weight_pieces(block):
        pieces = [
            (wqkv_hbm.at[0], wqkv.at[block]),
            (wout_hbm.at[0], wout.at[block]),
            (wup_hbm.at[0], wup.at[block]),
            (wdown_hbm.at[0], wdown.at[block]),
        ]
        return pieces

    own_pieces = weight_pieces(section)
    for i, (source, target) in enumerate(own_pieces):
        pltpu.make_async_copy(source, target, weight_sems.at[section, i]).start()

    def weight_sends():
        sends = []
        for n, other in enumerate(others):
            for i, (source, target) in enumerate(own_pieces):
                sends.append(
                    pltpu.make_async_remote_copy(
                        src_ref=source,
                        dst_ref=target,
                        send_sem=weight_send_sems.at[n, i],
                        recv_sem=weight_sems.at[section, i],
                        device_id={"section": other},
                        device_id_type=MESH,
                    )
                )
        return sends

    def wait_weight(block, i):
        target = weight_pieces(block)[i][1]
        pltpu.make_async_copy(target, target, weight_sems.at[block, i]).wait()

    def halo_send(block, way, part):
        span = pl.ds(part * chunk, chunk)
        return pltpu.make_async_remote_copy(
            src_ref=normed.at[block, 1 if way == 0 else near_slot, span],
            dst_ref=normed.at[block, far_slot, span],
            send_sem=halo_send_sems.at[block, way, part],
            recv_sem=halo_sems.at[block, way, part],
            device_id={"region": buddy if way == 0 else far_target},
            device_id_type=MESH,
        )

    order_copy.wait()
    slots = lax.broadcasted_iota(jnp.int32, (rows, rows), 0)
    picks = (slots == order_ref[...]).astype(jnp.float32).astype(jnp.bfloat16)
    hits_copy.wait()
    start = lax.dot_general(
        picks, hits_ref[...], (((0,), (0,)), ((), ())), preferred_element_type=jnp.float32
    )
    state[...] = start
    normed[0, 1] = normalize(start)
    links_copy.wait()
    counts_copy.wait()
    pl.semaphore_wait(barrier, segments + has_target.astype(jnp.int32))
    for part in range(HALO_PARTS):
        halo_send(0, 0, part).start()
    for send in weight_sends():
        send.start()

    lane = lax.broadcasted_iota(jnp.int32, (1, LANES), 1)
    head_lanes = [lane // head_width == j for j in range(group)]
    key_slot = lax.broadcasted_iota(jnp.int32, (1, patch_rows), 1)
    ones = jnp.ones((links_count * patch_rows, LANES), jnp.bfloat16)

    def near_pair(block, slot):
        both = product(
            normed[block, slot], wqkv[block, :, pl.ds(width, 2 * width)]
        ).astype(jnp.bfloat16)
        for i in range(patches):
            piece = both[i * patch_rows : (i + 1) * patch_rows]
            keys[slot * patches + i] = piece[:, :width]
            values[slot * patches + i] = piece[:, width:]

    def run_block(block, carry):
        wait_weight(block, 0)
        queries[...] = (
            product(normed[block, 1], wqkv[block, :, pl.ds(0, width)])
            * (math.log2(math.e) * head_width ** (-0.5))
        ).astype(jnp.bfloat16)
        near_pair(block, 1)

        for part in range(HALO_PARTS):
            halo_send(block, 0, part).wait_recv()

            @pl.when(has_target)
            def _():
                halo_send(block, 1, part).start()

        near_pair(block, near_slot)

        @pl.when(has_source)
        def _():
            for part in range(HALO_PARTS):
                halo_send(block, 1, part).wait_recv()

        @pl.when(jnp.logical_not(has_source))
        def _():
            normed[block, far_slot] = jnp.zeros((rows, width), jnp.bfloat16)

        near_pair(block, far_slot)

        masks, nears = [], []
        for patch in range(patches):
            linked = [links_ref[section, patch, j] for j in range(links_count)]
            nears.append(
                [jnp.clip(link - region * patches + REACH, 0, keys.shape[0] - 1) for link in linked]
            )
            masks.append(
                jnp.concatenate(
                    [
                        key_slot
                        < counts_ref[section, link // patches] - lax.rem(link, patches) * patch_rows
                        for link in linked
                    ],
                    axis=1,
                )
            )

        def patch_scores(patch, first):
            own = queries[pl.ds(patch * patch_rows, patch_rows), pl.ds(first, LANES)]
            stacked = jnp.concatenate(
                [jnp.where(chosen, own, jnp.zeros_like(own)) for chosen in head_lanes], axis=0
            )
            near_keys = jnp.concatenate(
                [keys[i, :, pl.ds(first, LANES)] for i in nears[patch]], axis=0
            )
            return lax.dot_general(
                stacked, near_keys, (((1,), (1,)), ((), ())), preferred_element_type=jnp.float32
            )

        steps = [(patch, first) for patch in range(patches) for first in range(0, width, LANES)]
        ahead = patch_scores(*steps[0])
        for n, (patch, first) in enumerate(steps):
            scores = ahead
            if n + 1 < len(steps):
                ahead = patch_scores(*steps[n + 1])
            scores = jnp.where(masks[patch], scores, -1e30)
            weights = jnp.exp2(scores - jnp.max(scores, axis=-1, keepdims=True)).astype(jnp.bfloat16)
            near_values = jnp.concatenate(
                [values[i, :, pl.ds(first, LANES)] for i in nears[patch]], axis=0
            )
            mixed = product(weights, jnp.concatenate([near_values, ones], axis=1))
            mixed = mixed[:, :LANES] * pl.reciprocal(mixed[:, LANES:], approx=True)
            result = mixed[:patch_rows]
            for j in range(1, group):
                result = jnp.where(
                    head_lanes[j], mixed[j * patch_rows : (j + 1) * patch_rows], result
                )
            attended[pl.ds(patch * patch_rows, patch_rows), pl.ds(first, LANES)] = result.astype(
                jnp.bfloat16
            )

        for i in range(1, 4):
            wait_weight(block, i)
        middle = (state[...] + product(attended[...], wout[block])).astype(jnp.bfloat16)
        middle = middle.astype(jnp.float32)
        normed_mlp = normalize(middle)
        total = middle
        ahead = product(normed_mlp, wup[block, :, pl.ds(0, ff_part)])
        for part in range(FF_PARTS):
            raised = ahead
            if part + 1 < FF_PARTS:
                ahead = product(normed_mlp, wup[block, :, pl.ds((part + 1) * ff_part, ff_part)])
            hidden = gelu(raised).astype(jnp.bfloat16)
            total = total + product(hidden, wdown[block, pl.ds(part * ff_part, ff_part), :])
        total = total.astype(jnp.bfloat16).astype(jnp.float32)
        state[...] = total

        @pl.when(block < segments - 1)
        def _():
            normed[block + 1, 1] = normalize(state[...])
            for part in range(HALO_PARTS):
                halo_send(block + 1, 0, part).start()

        for part in range(HALO_PARTS):
            halo_send(block, 0, part).wait_send()

        @pl.when(has_target)
        def _():
            for part in range(HALO_PARTS):
                halo_send(block, 1, part).wait_send()

        return carry

    lax.fori_loop(0, segments, run_block, 0)
    row = lax.broadcasted_iota(jnp.int32, (rows, 1), 0)
    kept = jnp.where(row < counts_ref[section, region], state[...], 0.0)
    out_ref[0] = kept
    for send in weight_sends():
        send.wait_send()


def per_device(hits, order, links, counts, w_qkv, w_out, w_up, w_down):
    segments = lax.axis_size("section")
    regions = lax.axis_size("region")
    rows, width = hits.shape[1:]
    patches = links.shape[1]
    patch_rows = rows // patches
    near_patches = patches + 2 * REACH
    assert patches == REACH and regions % 2 == 0 and w_qkv.shape[0] == 1
    piece_count = 4
    vmem = pl.BlockSpec(memory_space=pltpu.VMEM)
    hbm = pl.BlockSpec(memory_space=pltpu.HBM)
    bf16 = jnp.bfloat16
    encoded = pl.pallas_call(
        functools.partial(kernel, segments, regions),
        out_shape=jax.ShapeDtypeStruct((1, rows, width), jnp.float32),
        in_specs=[hbm] * 8,
        out_specs=vmem,
        scratch_shapes=[
            pltpu.VMEM((segments,) + w_qkv.shape[1:], bf16),
            pltpu.VMEM((segments,) + w_out.shape[1:], bf16),
            pltpu.VMEM((segments,) + w_up.shape[1:], bf16),
            pltpu.VMEM((segments,) + w_down.shape[1:], bf16),
            pltpu.VMEM((rows, width), jnp.float32),
            pltpu.VMEM((segments, 3, rows, width), bf16),
            pltpu.VMEM((rows, width), bf16),
            pltpu.VMEM((near_patches, patch_rows, width), bf16),
            pltpu.VMEM((near_patches, patch_rows, width), bf16),
            pltpu.VMEM((rows, width), bf16),
            pltpu.VMEM((rows, width), bf16),
            pltpu.VMEM(order.shape[1:], jnp.int32),
            pltpu.SMEM(links.shape, jnp.int32),
            pltpu.SMEM(counts.shape, jnp.int32),
            pltpu.SemaphoreType.DMA((4,)),
            pltpu.SemaphoreType.DMA((segments, piece_count)),
            pltpu.SemaphoreType.DMA((segments - 1, piece_count)),
            pltpu.SemaphoreType.DMA((segments, 2, HALO_PARTS)),
            pltpu.SemaphoreType.DMA((segments, 2, HALO_PARTS)),
        ],
        compiler_params=pltpu.CompilerParams(
            collective_id=0, has_side_effects=True, vmem_limit_bytes=60 * 2**20
        ),
        name="blocks",
    )(links, counts, hits, order, w_qkv, w_out, w_up, w_down)
    return encoded.astype(bf16)


def solution(mesh):
    in_specs = (
        P("section", "region", None),
        P(None, "region", None),
        P(None, "region", None),
        P(),
        P("section", None, None),
        P("section", None, None),
        P("section", None, None),
        P("section", None, None),
    )
    out_specs = P("section", "region", None)
    return jax.shard_map(
        per_device, mesh=mesh, in_specs=in_specs, out_specs=out_specs, check_vma=False
    )
```

```python
import functools
import math

import jax
import jax.numpy as jnp
from jax import lax
from jax.experimental import pallas as pl
from jax.experimental.pallas import tpu as pltpu
from jax.sharding import PartitionSpec as P

HEADS = 8
REACH = 2
FF_PARTS = 4
HALO_PARTS = 4
LANES = 128
epsilon = 1e-05
MESH = pl.DeviceIdType.MESH


def product(left, right):
    return jnp.dot(left, right, preferred_element_type=jnp.float32)


def normalize(values):
    center = jnp.mean(values, axis=-1, keepdims=True)
    moved = values - center
    spread = jnp.mean(moved * moved, axis=-1, keepdims=True)
    return (moved * lax.rsqrt(spread + epsilon)).astype(jnp.bfloat16)


def gelu(values):
    size = jnp.abs(values)
    t = pl.reciprocal(1.0 + (0.3275911 * 0.5**0.5) * size, approx=True)
    series = 1.061405429 * t - 1.453152027
    series = series * t + 1.421413741
    series = series * t - 0.284496736
    series = series * t + 0.254829592
    tail = (series * t) * jnp.exp(-0.5 * (values * values))
    return jnp.maximum(values, 0.0) - (0.5 * size) * tail


def kernel(
    segments,
    regions,
    links_hbm,
    counts_hbm,
    hits_hbm,
    order_hbm,
    wqkv_hbm,
    wout_hbm,
    wup_hbm,
    wdown_hbm,
    out_ref,
    wqkv,
    wout,
    wup,
    wdown,
    state,
    normed,
    queries,
    keys,
    values,
    attended,
    own_mixed,
    own_highest,
    hits_ref,
    order_ref,
    links_ref,
    counts_ref,
    input_sems,
    weight_sems,
    weight_send_sems,
    halo_sems,
    halo_send_sems,
):
    section = lax.axis_index("section")
    region = lax.axis_index("region")
    rows, width = state.shape
    patches = links_ref.shape[1]
    links_count = links_ref.shape[2]
    patch_rows = rows // patches
    chunk = rows // HALO_PARTS
    head_width = width // HEADS
    group = LANES // head_width
    ff_part = wup.shape[2] // FF_PARTS
    parity = lax.rem(region, 2)
    near_slot = 2 * (1 - parity)
    far_slot = 2 * parity
    buddy = region + 1 - 2 * parity
    far_target = region + 2 - 4 * parity
    far_source = region - 2 + 4 * parity
    has_target = jnp.logical_and(far_target >= 0, far_target < regions)
    has_source = jnp.logical_and(far_source >= 0, far_source < regions)
    others = [lax.rem(section + i, segments) for i in range(1, segments)]

    hits_copy = pltpu.make_async_copy(hits_hbm.at[0], hits_ref, input_sems.at[0])
    order_copy = pltpu.make_async_copy(order_hbm.at[section], order_ref, input_sems.at[1])
    links_copy = pltpu.make_async_copy(links_hbm, links_ref, input_sems.at[2])
    counts_copy = pltpu.make_async_copy(counts_hbm, counts_ref, input_sems.at[3])
    hits_copy.start()
    order_copy.start()
    links_copy.start()
    counts_copy.start()
    barrier = pltpu.get_barrier_semaphore()
    for other in others:
        pl.semaphore_signal(barrier, inc=1, device_id={"section": other}, device_id_type=MESH)

    pl.semaphore_signal(barrier, inc=1, device_id={"region": buddy}, device_id_type=MESH)

    @pl.when(has_source)
    def _():
        pl.semaphore_signal(barrier, inc=1, device_id={"region": far_source}, device_id_type=MESH)

    def weight_pieces(block):
        pieces = [
            (wqkv_hbm.at[0], wqkv.at[block]),
            (wout_hbm.at[0], wout.at[block]),
            (wup_hbm.at[0], wup.at[block]),
            (wdown_hbm.at[0], wdown.at[block]),
        ]
        return pieces

    own_pieces = weight_pieces(section)
    for i, (source, target) in enumerate(own_pieces):
        pltpu.make_async_copy(source, target, weight_sems.at[section, i]).start()

    def weight_sends():
        sends = []
        for n, other in enumerate(others):
            for i, (source, target) in enumerate(own_pieces):
                sends.append(
                    pltpu.make_async_remote_copy(
                        src_ref=source,
                        dst_ref=target,
                        send_sem=weight_send_sems.at[n, i],
                        recv_sem=weight_sems.at[section, i],
                        device_id={"section": other},
                        device_id_type=MESH,
                    )
                )
        return sends

    def wait_weight(block, i):
        target = weight_pieces(block)[i][1]
        pltpu.make_async_copy(target, target, weight_sems.at[block, i]).wait()

    def halo_send(block, way, part):
        span = pl.ds(part * chunk, chunk)
        return pltpu.make_async_remote_copy(
            src_ref=normed.at[block, 1 if way == 0 else near_slot, span],
            dst_ref=normed.at[block, far_slot, span],
            send_sem=halo_send_sems.at[block, way, part],
            recv_sem=halo_sems.at[block, way, part],
            device_id={"region": buddy if way == 0 else far_target},
            device_id_type=MESH,
        )

    order_copy.wait()
    slots = lax.broadcasted_iota(jnp.int32, (rows, rows), 0)
    picks = (slots == order_ref[...]).astype(jnp.float32).astype(jnp.bfloat16)
    hits_copy.wait()
    start = lax.dot_general(
        picks, hits_ref[...], (((0,), (0,)), ((), ())), preferred_element_type=jnp.float32
    )
    state[...] = start
    normed[0, 1] = normalize(start)
    links_copy.wait()
    counts_copy.wait()
    pl.semaphore_wait(barrier, segments + has_target.astype(jnp.int32))
    for part in range(HALO_PARTS):
        halo_send(0, 0, part).start()
    for send in weight_sends():
        send.start()

    lane = lax.broadcasted_iota(jnp.int32, (1, LANES), 1)
    head_lanes = [lane // head_width == j for j in range(group)]
    key_slot = lax.broadcasted_iota(jnp.int32, (1, patch_rows), 1)
    ones = jnp.ones((links_count * patch_rows, LANES), jnp.bfloat16)
    firsts = list(range(0, width, LANES))
    last = segments - 1
    per_patch = HALO_PARTS // patches

    def near_pair(block, slot):
        both = product(
            normed[block, slot], wqkv[block, :, pl.ds(width, 2 * width)]
        ).astype(jnp.bfloat16)
        for i in range(patches):
            piece = both[i * patch_rows : (i + 1) * patch_rows]
            keys[slot * patches + i] = piece[:, :width]
            values[slot * patches + i] = piece[:, width:]

    def key_mask(link):
        kept = counts_ref[section, link // patches] - lax.rem(link, patches) * patch_rows
        return key_slot < kept

    own_masks, masks, nears = [], [], []
    for patch in range(patches):
        linked = [links_ref[section, patch, j] for j in range(1, links_count)]
        nears.append(
            [jnp.clip(link - region * patches + REACH, 0, keys.shape[0] - 1) for link in linked]
        )
        masks.append(jnp.concatenate([key_mask(link) for link in linked], axis=1))
        own_masks.append(key_mask(region * patches + patch))

    def scores_of(patch, first, near):
        own = queries[pl.ds(patch * patch_rows, patch_rows), pl.ds(first, LANES)]
        stacked = jnp.concatenate(
            [jnp.where(chosen, own, jnp.zeros_like(own)) for chosen in head_lanes], axis=0
        )
        near_keys = jnp.concatenate([keys[i, :, pl.ds(first, LANES)] for i in near], axis=0)
        return lax.dot_general(
            stacked, near_keys, (((1,), (1,)), ((), ())), preferred_element_type=jnp.float32
        )

    def mix(weights, first, near):
        near_values = jnp.concatenate([values[i, :, pl.ds(first, LANES)] for i in near], axis=0)
        with_ones = jnp.concatenate([near_values, ones[: near_values.shape[0]]], axis=1)
        return product(weights.astype(jnp.bfloat16), with_ones)

    def attend_own(patch):
        near = [patches + patch]
        ahead = scores_of(patch, firsts[0], near)
        for n, first in enumerate(firsts):
            scores = ahead
            if n + 1 < len(firsts):
                ahead = scores_of(patch, firsts[n + 1], near)
            scores = jnp.where(own_masks[patch], scores, -1e30)
            highest = jnp.max(scores, axis=-1, keepdims=True)
            own_highest[patch * len(firsts) + n] = highest
            own_mixed[patch * len(firsts) + n] = mix(jnp.exp2(scores - highest), first, near)

    def attend(patch):
        near = nears[patch]
        span = pl.ds(patch * patch_rows, patch_rows)
        ahead = scores_of(patch, firsts[0], near)
        for n, first in enumerate(firsts):
            scores = ahead
            if n + 1 < len(firsts):
                ahead = scores_of(patch, firsts[n + 1], near)
            scores = jnp.where(masks[patch], scores, -1e30)
            before = own_highest[patch * len(firsts) + n]
            highest = jnp.maximum(before, jnp.max(scores, axis=-1, keepdims=True))
            mixed = mix(jnp.exp2(scores - highest), first, near)
            mixed = mixed + own_mixed[patch * len(firsts) + n] * jnp.exp2(before - highest)
            mixed = mixed[:, :LANES] * pl.reciprocal(mixed[:, LANES:], approx=True)
            result = mixed[:patch_rows]
            for j in range(1, group):
                result = jnp.where(
                    head_lanes[j], mixed[j * patch_rows : (j + 1) * patch_rows], result
                )
            attended[span, pl.ds(first, LANES)] = result.astype(jnp.bfloat16)

    def feed_forward(block, start_row, count):
        span = pl.ds(start_row, count)
        middle = (state[span, :] + product(attended[span, :], wout[block])).astype(jnp.bfloat16)
        middle = middle.astype(jnp.float32)
        normed_mlp = normalize(middle)
        total = middle
        ahead = product(normed_mlp, wup[block, :, pl.ds(0, ff_part)])
        for part in range(FF_PARTS):
            raised = ahead
            if part + 1 < FF_PARTS:
                ahead = product(normed_mlp, wup[block, :, pl.ds((part + 1) * ff_part, ff_part)])
            hidden = gelu(raised).astype(jnp.bfloat16)
            total = total + product(hidden, wdown[block, pl.ds(part * ff_part, ff_part), :])
        return total.astype(jnp.bfloat16).astype(jnp.float32)

    def pass_on(block, part):
        halo_send(block, 0, part).wait_recv()

        @pl.when(has_target)
        def _():
            halo_send(block, 1, part).start()

    for block in range(segments):
        first_parts = per_patch if block > 0 else 0
        for part in range(first_parts):
            pass_on(block, part)
        wait_weight(block, 0)
        queries[...] = (
            product(normed[block, 1], wqkv[block, :, pl.ds(0, width)])
            * (math.log2(math.e) * head_width ** (-0.5))
        ).astype(jnp.bfloat16)
        near_pair(block, 1)
        later = list(range(first_parts, HALO_PARTS))
        for patch in range(patches):
            pass_on(block, later.pop(0))
            attend_own(patch)
        for part in later:
            pass_on(block, part)
        near_pair(block, near_slot)

        @pl.when(has_source)
        def _():
            for part in range(HALO_PARTS):
                halo_send(block, 1, part).wait_recv()

        @pl.when(jnp.logical_not(has_source))
        def _():
            normed[block, far_slot] = jnp.zeros((rows, width), jnp.bfloat16)

        near_pair(block, far_slot)
        for i in range(1, 4):
            wait_weight(block, i)
        if block < last:
            for patch in range(patches):
                attend(patch)
                start_row = patch * patch_rows
                total = feed_forward(block, start_row, patch_rows)
                state[pl.ds(start_row, patch_rows), :] = total
                normed[block + 1, 1, pl.ds(start_row, patch_rows), :] = normalize(total)
                for part in range(patch * per_patch, (patch + 1) * per_patch):
                    halo_send(block + 1, 0, part).start()
        else:
            for patch in range(patches):
                attend(patch)
            state[...] = feed_forward(block, 0, rows)

    row = lax.broadcasted_iota(jnp.int32, (rows, 1), 0)
    kept = jnp.where(row < counts_ref[section, region], state[...], 0.0)
    out_ref[0] = kept
    for block in range(segments):
        for part in range(HALO_PARTS):
            halo_send(block, 0, part).wait_send()

        @pl.when(has_target)
        def _():
            for part in range(HALO_PARTS):
                halo_send(block, 1, part).wait_send()

    for send in weight_sends():
        send.wait_send()


def per_device(hits, order, links, counts, w_qkv, w_out, w_up, w_down):
    segments = lax.axis_size("section")
    regions = lax.axis_size("region")
    rows, width = hits.shape[1:]
    patches = links.shape[1]
    patch_rows = rows // patches
    near_patches = patches + 2 * REACH
    group = LANES * HEADS // width
    assert patches == REACH and regions % 2 == 0 and w_qkv.shape[0] == 1
    piece_count = 4
    vmem = pl.BlockSpec(memory_space=pltpu.VMEM)
    hbm = pl.BlockSpec(memory_space=pltpu.HBM)
    bf16 = jnp.bfloat16
    encoded = pl.pallas_call(
        functools.partial(kernel, segments, regions),
        out_shape=jax.ShapeDtypeStruct((1, rows, width), jnp.float32),
        in_specs=[hbm] * 8,
        out_specs=vmem,
        scratch_shapes=[
            pltpu.VMEM((segments,) + w_qkv.shape[1:], bf16),
            pltpu.VMEM((segments,) + w_out.shape[1:], bf16),
            pltpu.VMEM((segments,) + w_up.shape[1:], bf16),
            pltpu.VMEM((segments,) + w_down.shape[1:], bf16),
            pltpu.VMEM((rows, width), jnp.float32),
            pltpu.VMEM((segments, 3, rows, width), bf16),
            pltpu.VMEM((rows, width), bf16),
            pltpu.VMEM((near_patches, patch_rows, width), bf16),
            pltpu.VMEM((near_patches, patch_rows, width), bf16),
            pltpu.VMEM((rows, width), bf16),
            pltpu.VMEM((patches * (width // LANES), group * patch_rows, 2 * LANES), jnp.float32),
            pltpu.VMEM((patches * (width // LANES), group * patch_rows, 1), jnp.float32),
            pltpu.VMEM((rows, width), bf16),
            pltpu.VMEM(order.shape[1:], jnp.int32),
            pltpu.SMEM(links.shape, jnp.int32),
            pltpu.SMEM(counts.shape, jnp.int32),
            pltpu.SemaphoreType.DMA((4,)),
            pltpu.SemaphoreType.DMA((segments, piece_count)),
            pltpu.SemaphoreType.DMA((segments - 1, piece_count)),
            pltpu.SemaphoreType.DMA((segments, 2, HALO_PARTS)),
            pltpu.SemaphoreType.DMA((segments, 2, HALO_PARTS)),
        ],
        compiler_params=pltpu.CompilerParams(
            collective_id=0, has_side_effects=True, vmem_limit_bytes=60 * 2**20
        ),
        name="blocks",
    )(links, counts, hits, order, w_qkv, w_out, w_up, w_down)
    return encoded.astype(bf16)


def solution(mesh):
    in_specs = (
        P("section", "region", None),
        P(None, "region", None),
        P(None, "region", None),
        P(),
        P("section", None, None),
        P("section", None, None),
        P("section", None, None),
        P("section", None, None),
    )
    out_specs = P("section", "region", None)
    return jax.shard_map(
        per_device, mesh=mesh, in_specs=in_specs, out_specs=out_specs, check_vma=False
    )
```

```python
import functools
import math

import jax
import jax.numpy as jnp
from jax import lax
from jax.experimental import pallas as pl
from jax.experimental.pallas import tpu as pltpu
from jax.sharding import PartitionSpec as P

HEADS = 8
REACH = 2
FF_PARTS = 4
HALO_PARTS = 8
LANES = 128
epsilon = 1e-05
MESH = pl.DeviceIdType.MESH


def product(left, right):
    return jnp.dot(left, right, preferred_element_type=jnp.float32)


def normalize(values):
    center = jnp.mean(values, axis=-1, keepdims=True)
    moved = values - center
    spread = jnp.mean(moved * moved, axis=-1, keepdims=True)
    return (moved * lax.rsqrt(spread + epsilon)).astype(jnp.bfloat16)


def gelu(values):
    size = jnp.abs(values)
    t = pl.reciprocal(1.0 + (0.3275911 * 0.5**0.5) * size, approx=True)
    series = 1.061405429 * t - 1.453152027
    series = series * t + 1.421413741
    series = series * t - 0.284496736
    series = series * t + 0.254829592
    tail = (series * t) * jnp.exp(-0.5 * (values * values))
    return jnp.maximum(values, 0.0) - (0.5 * size) * tail


def kernel(
    segments,
    regions,
    links_hbm,
    counts_hbm,
    hits_hbm,
    order_hbm,
    wqkv_hbm,
    wout_hbm,
    wup_hbm,
    wdown_hbm,
    out_ref,
    wqkv,
    wout,
    wup,
    wdown,
    state,
    normed,
    queries,
    keys,
    values,
    attended,
    own_mixed,
    own_highest,
    hits_ref,
    order_ref,
    links_ref,
    counts_ref,
    input_sems,
    weight_sems,
    weight_send_sems,
    halo_sems,
    halo_send_sems,
):
    section = lax.axis_index("section")
    region = lax.axis_index("region")
    rows, width = state.shape
    patches = links_ref.shape[1]
    links_count = links_ref.shape[2]
    patch_rows = rows // patches
    chunk = rows // HALO_PARTS
    head_width = width // HEADS
    group = LANES // head_width
    ff_part = wup.shape[2] // FF_PARTS
    parity = lax.rem(region, 2)
    near_slot = 2 * (1 - parity)
    far_slot = 2 * parity
    buddy = region + 1 - 2 * parity
    far_target = region + 2 - 4 * parity
    far_source = region - 2 + 4 * parity
    has_target = jnp.logical_and(far_target >= 0, far_target < regions)
    has_source = jnp.logical_and(far_source >= 0, far_source < regions)
    others = [lax.rem(section + i, segments) for i in range(1, segments)]

    hits_copy = pltpu.make_async_copy(hits_hbm.at[0], hits_ref, input_sems.at[0])
    order_copy = pltpu.make_async_copy(order_hbm.at[section], order_ref, input_sems.at[1])
    links_copy = pltpu.make_async_copy(links_hbm, links_ref, input_sems.at[2])
    counts_copy = pltpu.make_async_copy(counts_hbm, counts_ref, input_sems.at[3])
    hits_copy.start()
    order_copy.start()
    links_copy.start()
    counts_copy.start()
    barrier = pltpu.get_barrier_semaphore()
    for other in others:
        pl.semaphore_signal(barrier, inc=1, device_id={"section": other}, device_id_type=MESH)

    pl.semaphore_signal(barrier, inc=1, device_id={"region": buddy}, device_id_type=MESH)

    @pl.when(has_source)
    def _():
        pl.semaphore_signal(barrier, inc=1, device_id={"region": far_source}, device_id_type=MESH)

    def weight_pieces(block):
        pieces = [
            (wqkv_hbm.at[0], wqkv.at[block]),
            (wout_hbm.at[0], wout.at[block]),
            (wup_hbm.at[0], wup.at[block]),
            (wdown_hbm.at[0], wdown.at[block]),
        ]
        return pieces

    own_pieces = weight_pieces(section)
    for i, (source, target) in enumerate(own_pieces):
        pltpu.make_async_copy(source, target, weight_sems.at[section, i]).start()

    def weight_sends():
        sends = []
        for n, other in enumerate(others):
            for i, (source, target) in enumerate(own_pieces):
                sends.append(
                    pltpu.make_async_remote_copy(
                        src_ref=source,
                        dst_ref=target,
                        send_sem=weight_send_sems.at[n, i],
                        recv_sem=weight_sems.at[section, i],
                        device_id={"section": other},
                        device_id_type=MESH,
                    )
                )
        return sends

    def wait_weight(block, i):
        target = weight_pieces(block)[i][1]
        pltpu.make_async_copy(target, target, weight_sems.at[block, i]).wait()

    def halo_send(block, way, part):
        span = pl.ds(part * chunk, chunk)
        return pltpu.make_async_remote_copy(
            src_ref=normed.at[block, 1 if way == 0 else near_slot, span],
            dst_ref=normed.at[block, far_slot, span],
            send_sem=halo_send_sems.at[block, way, part],
            recv_sem=halo_sems.at[block, way, part],
            device_id={"region": buddy if way == 0 else far_target},
            device_id_type=MESH,
        )

    order_copy.wait()
    slots = lax.broadcasted_iota(jnp.int32, (rows, rows), 0)
    picks = (slots == order_ref[...]).astype(jnp.float32).astype(jnp.bfloat16)
    hits_copy.wait()
    start = lax.dot_general(
        picks, hits_ref[...], (((0,), (0,)), ((), ())), preferred_element_type=jnp.float32
    )
    state[...] = start
    normed[0, 1] = normalize(start)
    links_copy.wait()
    counts_copy.wait()
    pl.semaphore_wait(barrier, segments + has_target.astype(jnp.int32))
    for part in range(HALO_PARTS):
        halo_send(0, 0, part).start()
    for send in weight_sends():
        send.start()

    lane = lax.broadcasted_iota(jnp.int32, (1, LANES), 1)
    head_lanes = [lane // head_width == j for j in range(group)]
    key_slot = lax.broadcasted_iota(jnp.int32, (1, patch_rows), 1)
    ones = jnp.ones((links_count * patch_rows, LANES), jnp.bfloat16)
    firsts = list(range(0, width, LANES))
    last = segments - 1
    per_patch = HALO_PARTS // patches

    def near_pair(block, slot, first, count):
        both = product(
            normed[block, slot, pl.ds(first * patch_rows, count * patch_rows), :],
            wqkv[block, :, pl.ds(width, 2 * width)],
        ).astype(jnp.bfloat16)
        for i in range(count):
            piece = both[i * patch_rows : (i + 1) * patch_rows]
            keys[slot * patches + first + i] = piece[:, :width]
            values[slot * patches + first + i] = piece[:, width:]

    def key_mask(link):
        kept = counts_ref[section, link // patches] - lax.rem(link, patches) * patch_rows
        return key_slot < kept

    own_masks, masks, nears = [], [], []
    for patch in range(patches):
        linked = [links_ref[section, patch, j] for j in range(1, links_count)]
        nears.append(
            [jnp.clip(link - region * patches + REACH, 0, keys.shape[0] - 1) for link in linked]
        )
        masks.append(jnp.concatenate([key_mask(link) for link in linked], axis=1))
        own_masks.append(key_mask(region * patches + patch))

    def scores_of(patch, first, near):
        own = queries[pl.ds(patch * patch_rows, patch_rows), pl.ds(first, LANES)]
        stacked = jnp.concatenate(
            [jnp.where(chosen, own, jnp.zeros_like(own)) for chosen in head_lanes], axis=0
        )
        near_keys = jnp.concatenate([keys[i, :, pl.ds(first, LANES)] for i in near], axis=0)
        return lax.dot_general(
            stacked, near_keys, (((1,), (1,)), ((), ())), preferred_element_type=jnp.float32
        )

    def mix(weights, first, near):
        near_values = jnp.concatenate([values[i, :, pl.ds(first, LANES)] for i in near], axis=0)
        with_ones = jnp.concatenate([near_values, ones[: near_values.shape[0]]], axis=1)
        return product(weights.astype(jnp.bfloat16), with_ones)

    def attend_own(patch):
        near = [patches + patch]
        ahead = scores_of(patch, firsts[0], near)
        for n, first in enumerate(firsts):
            scores = ahead
            if n + 1 < len(firsts):
                ahead = scores_of(patch, firsts[n + 1], near)
            scores = jnp.where(own_masks[patch], scores, -1e30)
            highest = jnp.max(scores, axis=-1, keepdims=True)
            own_highest[patch * len(firsts) + n] = highest
            own_mixed[patch * len(firsts) + n] = mix(jnp.exp2(scores - highest), first, near)

    def attend(patch):
        near = nears[patch]
        span = pl.ds(patch * patch_rows, patch_rows)
        ahead = scores_of(patch, firsts[0], near)
        for n, first in enumerate(firsts):
            scores = ahead
            if n + 1 < len(firsts):
                ahead = scores_of(patch, firsts[n + 1], near)
            scores = jnp.where(masks[patch], scores, -1e30)
            before = own_highest[patch * len(firsts) + n]
            highest = jnp.maximum(before, jnp.max(scores, axis=-1, keepdims=True))
            mixed = mix(jnp.exp2(scores - highest), first, near)
            mixed = mixed + own_mixed[patch * len(firsts) + n] * jnp.exp2(before - highest)
            mixed = mixed[:, :LANES] * pl.reciprocal(mixed[:, LANES:], approx=True)
            result = mixed[:patch_rows]
            for j in range(1, group):
                result = jnp.where(
                    head_lanes[j], mixed[j * patch_rows : (j + 1) * patch_rows], result
                )
            attended[span, pl.ds(first, LANES)] = result.astype(jnp.bfloat16)

    def feed_forward(block, start_row, count):
        span = pl.ds(start_row, count)
        middle = (state[span, :] + product(attended[span, :], wout[block])).astype(jnp.bfloat16)
        middle = middle.astype(jnp.float32)
        normed_mlp = normalize(middle)
        total = middle
        ahead = product(normed_mlp, wup[block, :, pl.ds(0, ff_part)])
        for part in range(FF_PARTS):
            raised = ahead
            if part + 1 < FF_PARTS:
                ahead = product(normed_mlp, wup[block, :, pl.ds((part + 1) * ff_part, ff_part)])
            hidden = gelu(raised).astype(jnp.bfloat16)
            total = total + product(hidden, wdown[block, pl.ds(part * ff_part, ff_part), :])
        return total.astype(jnp.bfloat16).astype(jnp.float32)

    def pass_on(block, part):
        halo_send(block, 0, part).wait_recv()

        @pl.when(has_target)
        def _():
            halo_send(block, 1, part).start()

    for block in range(segments):
        first_parts = per_patch if block > 0 else 0
        for part in range(first_parts):
            pass_on(block, part)
        wait_weight(block, 0)
        queries[...] = (
            product(normed[block, 1], wqkv[block, :, pl.ds(0, width)])
            * (math.log2(math.e) * head_width ** (-0.5))
        ).astype(jnp.bfloat16)
        near_pair(block, 1, 0, patches)
        later = list(range(first_parts, HALO_PARTS))
        turn = len(later) // (patches + 1)
        for patch in range(patches):
            for part in later[:turn]:
                pass_on(block, part)
            later = later[turn:]
            attend_own(patch)
        for part in later:
            pass_on(block, part)
        near_pair(block, near_slot, 0, patches)

        @pl.when(jnp.logical_not(has_source))
        def _():
            normed[block, far_slot] = jnp.zeros((rows, width), jnp.bfloat16)

        for patch in range(patches):

            @pl.when(has_source)
            def _():
                for part in range(patch * per_patch, (patch + 1) * per_patch):
                    halo_send(block, 1, part).wait_recv()

            near_pair(block, far_slot, patch, 1)
        for i in range(1, 4):
            wait_weight(block, i)
        if block < last:
            for patch in range(patches):
                attend(patch)
                start_row = patch * patch_rows
                total = feed_forward(block, start_row, patch_rows)
                state[pl.ds(start_row, patch_rows), :] = total
                normed[block + 1, 1, pl.ds(start_row, patch_rows), :] = normalize(total)
                for part in range(patch * per_patch, (patch + 1) * per_patch):
                    halo_send(block + 1, 0, part).start()
        else:
            for patch in range(patches):
                attend(patch)
            state[...] = feed_forward(block, 0, rows)

    row = lax.broadcasted_iota(jnp.int32, (rows, 1), 0)
    kept = jnp.where(row < counts_ref[section, region], state[...], 0.0)
    out_ref[0] = kept
    for block in range(segments):
        for part in range(HALO_PARTS):
            halo_send(block, 0, part).wait_send()

        @pl.when(has_target)
        def _():
            for part in range(HALO_PARTS):
                halo_send(block, 1, part).wait_send()

    for send in weight_sends():
        send.wait_send()


def per_device(hits, order, links, counts, w_qkv, w_out, w_up, w_down):
    segments = lax.axis_size("section")
    regions = lax.axis_size("region")
    rows, width = hits.shape[1:]
    patches = links.shape[1]
    patch_rows = rows // patches
    near_patches = patches + 2 * REACH
    group = LANES * HEADS // width
    assert patches == REACH and regions % 2 == 0 and w_qkv.shape[0] == 1
    piece_count = 4
    vmem = pl.BlockSpec(memory_space=pltpu.VMEM)
    hbm = pl.BlockSpec(memory_space=pltpu.HBM)
    bf16 = jnp.bfloat16
    encoded = pl.pallas_call(
        functools.partial(kernel, segments, regions),
        out_shape=jax.ShapeDtypeStruct((1, rows, width), jnp.float32),
        in_specs=[hbm] * 8,
        out_specs=vmem,
        scratch_shapes=[
            pltpu.VMEM((segments,) + w_qkv.shape[1:], bf16),
            pltpu.VMEM((segments,) + w_out.shape[1:], bf16),
            pltpu.VMEM((segments,) + w_up.shape[1:], bf16),
            pltpu.VMEM((segments,) + w_down.shape[1:], bf16),
            pltpu.VMEM((rows, width), jnp.float32),
            pltpu.VMEM((segments, 3, rows, width), bf16),
            pltpu.VMEM((rows, width), bf16),
            pltpu.VMEM((near_patches, patch_rows, width), bf16),
            pltpu.VMEM((near_patches, patch_rows, width), bf16),
            pltpu.VMEM((rows, width), bf16),
            pltpu.VMEM((patches * (width // LANES), group * patch_rows, 2 * LANES), jnp.float32),
            pltpu.VMEM((patches * (width // LANES), group * patch_rows, 1), jnp.float32),
            pltpu.VMEM((rows, width), bf16),
            pltpu.VMEM(order.shape[1:], jnp.int32),
            pltpu.SMEM(links.shape, jnp.int32),
            pltpu.SMEM(counts.shape, jnp.int32),
            pltpu.SemaphoreType.DMA((4,)),
            pltpu.SemaphoreType.DMA((segments, piece_count)),
            pltpu.SemaphoreType.DMA((segments - 1, piece_count)),
            pltpu.SemaphoreType.DMA((segments, 2, HALO_PARTS)),
            pltpu.SemaphoreType.DMA((segments, 2, HALO_PARTS)),
        ],
        compiler_params=pltpu.CompilerParams(
            collective_id=0, has_side_effects=True, vmem_limit_bytes=60 * 2**20
        ),
        name="blocks",
    )(links, counts, hits, order, w_qkv, w_out, w_up, w_down)
    return encoded.astype(bf16)


def solution(mesh):
    in_specs = (
        P("section", "region", None),
        P(None, "region", None),
        P(None, "region", None),
        P(),
        P("section", None, None),
        P("section", None, None),
        P("section", None, None),
        P("section", None, None),
    )
    out_specs = P("section", "region", None)
    return jax.shard_map(
        per_device, mesh=mesh, in_specs=in_specs, out_specs=out_specs, check_vma=False
    )
```

```python
import functools
import math

import jax
import jax.numpy as jnp
from jax import lax
from jax.experimental import pallas as pl
from jax.experimental.pallas import tpu as pltpu
from jax.sharding import PartitionSpec as P

HEADS = 8
REACH = 2
FF_PARTS = 4
HALO_PARTS = 8
LANES = 128
epsilon = 1e-05
MESH = pl.DeviceIdType.MESH


def product(left, right):
    return jnp.dot(left, right, preferred_element_type=jnp.float32)


def normalize(values):
    center = jnp.mean(values, axis=-1, keepdims=True)
    moved = values - center
    spread = jnp.mean(moved * moved, axis=-1, keepdims=True)
    return (moved * lax.rsqrt(spread + epsilon)).astype(jnp.bfloat16)


def gelu(values):
    size = jnp.abs(values)
    t = pl.reciprocal(1.0 + (0.3275911 * 0.5**0.5) * size, approx=True)
    series = 1.061405429 * t - 1.453152027
    series = series * t + 1.421413741
    series = series * t - 0.284496736
    series = series * t + 0.254829592
    tail = (series * t) * jnp.exp(-0.5 * (values * values))
    return jnp.maximum(values, 0.0) - (0.5 * size) * tail


def kernel(
    segments,
    regions,
    links_hbm,
    counts_hbm,
    hits_hbm,
    order_hbm,
    wqkv_hbm,
    wout_hbm,
    wup_hbm,
    wdown_hbm,
    out_ref,
    wqkv,
    wout,
    wup,
    wdown,
    state,
    normed,
    queries,
    keys,
    values,
    attended,
    own_mixed,
    own_highest,
    hits_ref,
    order_ref,
    links_ref,
    counts_ref,
    input_sems,
    weight_sems,
    weight_send_sems,
    halo_sems,
    halo_send_sems,
):
    section = lax.axis_index("section")
    region = lax.axis_index("region")
    rows, width = state.shape
    patches = links_ref.shape[1]
    links_count = links_ref.shape[2]
    patch_rows = rows // patches
    chunk = rows // HALO_PARTS
    head_width = width // HEADS
    group = LANES // head_width
    ff_part = wup.shape[2] // FF_PARTS
    parity = lax.rem(region, 2)
    near_slot = 2 * (1 - parity)
    far_slot = 2 * parity
    buddy = region + 1 - 2 * parity
    far_target = region + 2 - 4 * parity
    far_source = region - 2 + 4 * parity
    has_target = jnp.logical_and(far_target >= 0, far_target < regions)
    has_source = jnp.logical_and(far_source >= 0, far_source < regions)
    others = [lax.rem(section + i, segments) for i in range(1, segments)]

    hits_copy = pltpu.make_async_copy(hits_hbm.at[0], hits_ref, input_sems.at[0])
    order_copy = pltpu.make_async_copy(order_hbm.at[section], order_ref, input_sems.at[1])
    links_copy = pltpu.make_async_copy(links_hbm, links_ref, input_sems.at[2])
    counts_copy = pltpu.make_async_copy(counts_hbm, counts_ref, input_sems.at[3])
    hits_copy.start()
    order_copy.start()
    links_copy.start()
    counts_copy.start()
    barrier = pltpu.get_barrier_semaphore()
    for other in others:
        pl.semaphore_signal(barrier, inc=1, device_id={"section": other}, device_id_type=MESH)

    pl.semaphore_signal(barrier, inc=1, device_id={"region": buddy}, device_id_type=MESH)

    @pl.when(has_source)
    def _():
        pl.semaphore_signal(barrier, inc=1, device_id={"region": far_source}, device_id_type=MESH)

    def weight_pieces(block):
        pieces = [
            (wqkv_hbm.at[0], wqkv.at[block]),
            (wout_hbm.at[0], wout.at[block]),
            (wup_hbm.at[0], wup.at[block]),
            (wdown_hbm.at[0], wdown.at[block]),
        ]
        return pieces

    own_pieces = weight_pieces(section)
    for i, (source, target) in enumerate(own_pieces):
        pltpu.make_async_copy(source, target, weight_sems.at[section, i]).start()

    def weight_sends():
        sends = []
        for n, other in enumerate(others):
            for i, (source, target) in enumerate(own_pieces):
                sends.append(
                    pltpu.make_async_remote_copy(
                        src_ref=source,
                        dst_ref=target,
                        send_sem=weight_send_sems.at[n, i],
                        recv_sem=weight_sems.at[section, i],
                        device_id={"section": other},
                        device_id_type=MESH,
                    )
                )
        return sends

    def wait_weight(block, i):
        target = weight_pieces(block)[i][1]
        pltpu.make_async_copy(target, target, weight_sems.at[block, i]).wait()

    def halo_send(block, way, part):
        span = pl.ds(part * chunk, chunk)
        return pltpu.make_async_remote_copy(
            src_ref=normed.at[block, 1 if way == 0 else near_slot, span],
            dst_ref=normed.at[block, far_slot, span],
            send_sem=halo_send_sems.at[block, way, part],
            recv_sem=halo_sems.at[block, way, part],
            device_id={"region": buddy if way == 0 else far_target},
            device_id_type=MESH,
        )

    order_copy.wait()
    slots = lax.broadcasted_iota(jnp.int32, (rows, rows), 0)
    picks = (slots == order_ref[...]).astype(jnp.float32).astype(jnp.bfloat16)
    hits_copy.wait()
    for patch in range(patches):
        span = pl.ds(patch * patch_rows, patch_rows)
        start = lax.dot_general(
            picks[:, patch * patch_rows : (patch + 1) * patch_rows],
            hits_ref[...],
            (((0,), (0,)), ((), ())),
            preferred_element_type=jnp.float32,
        )
        state[span, :] = start
        normed[0, 1, span, :] = normalize(start)
        if patch == 0:
            links_copy.wait()
            counts_copy.wait()
            pl.semaphore_wait(barrier, segments + has_target.astype(jnp.int32))
        for part in range(patch * HALO_PARTS // patches, (patch + 1) * HALO_PARTS // patches):
            halo_send(0, 0, part).start()
    for send in weight_sends():
        send.start()

    lane = lax.broadcasted_iota(jnp.int32, (1, LANES), 1)
    head_lanes = [lane // head_width == j for j in range(group)]
    key_slot = lax.broadcasted_iota(jnp.int32, (1, patch_rows), 1)
    ones = jnp.ones((links_count * patch_rows, LANES), jnp.bfloat16)
    firsts = list(range(0, width, LANES))
    last = segments - 1
    per_patch = HALO_PARTS // patches

    def near_pair(block, slot, first, count):
        both = product(
            normed[block, slot, pl.ds(first * patch_rows, count * patch_rows), :],
            wqkv[block, :, pl.ds(width, 2 * width)],
        ).astype(jnp.bfloat16)
        for i in range(count):
            piece = both[i * patch_rows : (i + 1) * patch_rows]
            keys[slot * patches + first + i] = piece[:, :width]
            values[slot * patches + first + i] = piece[:, width:]

    def key_mask(link):
        kept = counts_ref[section, link // patches] - lax.rem(link, patches) * patch_rows
        return key_slot < kept

    own_masks, masks, nears = [], [], []
    for patch in range(patches):
        linked = [links_ref[section, patch, j] for j in range(1, links_count)]
        nears.append(
            [jnp.clip(link - region * patches + REACH, 0, keys.shape[0] - 1) for link in linked]
        )
        masks.append(jnp.concatenate([key_mask(link) for link in linked], axis=1))
        own_masks.append(key_mask(region * patches + patch))

    def scores_of(patch, first, near):
        own = queries[pl.ds(patch * patch_rows, patch_rows), pl.ds(first, LANES)]
        stacked = jnp.concatenate(
            [jnp.where(chosen, own, jnp.zeros_like(own)) for chosen in head_lanes], axis=0
        )
        near_keys = jnp.concatenate([keys[i, :, pl.ds(first, LANES)] for i in near], axis=0)
        return lax.dot_general(
            stacked, near_keys, (((1,), (1,)), ((), ())), preferred_element_type=jnp.float32
        )

    def mix(weights, first, near):
        near_values = jnp.concatenate([values[i, :, pl.ds(first, LANES)] for i in near], axis=0)
        with_ones = jnp.concatenate([near_values, ones[: near_values.shape[0]]], axis=1)
        return product(weights.astype(jnp.bfloat16), with_ones)

    def attend_own(patch):
        near = [patches + patch]
        ahead = scores_of(patch, firsts[0], near)
        for n, first in enumerate(firsts):
            scores = ahead
            if n + 1 < len(firsts):
                ahead = scores_of(patch, firsts[n + 1], near)
            scores = jnp.where(own_masks[patch], scores, -1e30)
            highest = jnp.max(scores, axis=-1, keepdims=True)
            own_highest[patch * len(firsts) + n] = highest
            own_mixed[patch * len(firsts) + n] = mix(jnp.exp2(scores - highest), first, near)

    def attend(patch):
        near = nears[patch]
        span = pl.ds(patch * patch_rows, patch_rows)
        ahead = scores_of(patch, firsts[0], near)
        for n, first in enumerate(firsts):
            scores = ahead
            if n + 1 < len(firsts):
                ahead = scores_of(patch, firsts[n + 1], near)
            scores = jnp.where(masks[patch], scores, -1e30)
            before = own_highest[patch * len(firsts) + n]
            highest = jnp.maximum(before, jnp.max(scores, axis=-1, keepdims=True))
            mixed = mix(jnp.exp2(scores - highest), first, near)
            mixed = mixed + own_mixed[patch * len(firsts) + n] * jnp.exp2(before - highest)
            mixed = mixed[:, :LANES] * pl.reciprocal(mixed[:, LANES:], approx=True)
            result = mixed[:patch_rows]
            for j in range(1, group):
                result = jnp.where(
                    head_lanes[j], mixed[j * patch_rows : (j + 1) * patch_rows], result
                )
            attended[span, pl.ds(first, LANES)] = result.astype(jnp.bfloat16)

    def feed_forward(block, start_row, count):
        span = pl.ds(start_row, count)
        middle = (state[span, :] + product(attended[span, :], wout[block])).astype(jnp.bfloat16)
        middle = middle.astype(jnp.float32)
        normed_mlp = normalize(middle)
        total = middle
        ahead = product(normed_mlp, wup[block, :, pl.ds(0, ff_part)])
        for part in range(FF_PARTS):
            raised = ahead
            if part + 1 < FF_PARTS:
                ahead = product(normed_mlp, wup[block, :, pl.ds((part + 1) * ff_part, ff_part)])
            hidden = gelu(raised).astype(jnp.bfloat16)
            total = total + product(hidden, wdown[block, pl.ds(part * ff_part, ff_part), :])
        return total.astype(jnp.bfloat16).astype(jnp.float32)

    def pass_on(block, part):
        halo_send(block, 0, part).wait_recv()

        @pl.when(has_target)
        def _():
            halo_send(block, 1, part).start()

    for block in range(segments):
        first_parts = per_patch if block > 0 else 0
        for part in range(first_parts):
            pass_on(block, part)
        wait_weight(block, 0)
        queries[...] = (
            product(normed[block, 1], wqkv[block, :, pl.ds(0, width)])
            * (math.log2(math.e) * head_width ** (-0.5))
        ).astype(jnp.bfloat16)
        near_pair(block, 1, 0, patches)
        later = list(range(first_parts, HALO_PARTS))
        turn = len(later) // (patches + 1)
        for patch in range(patches):
            for part in later[:turn]:
                pass_on(block, part)
            later = later[turn:]
            attend_own(patch)
        for part in later:
            pass_on(block, part)
        near_pair(block, near_slot, 0, patches)

        @pl.when(jnp.logical_not(has_source))
        def _():
            normed[block, far_slot] = jnp.zeros((rows, width), jnp.bfloat16)

        for patch in range(patches):

            @pl.when(has_source)
            def _():
                for part in range(patch * per_patch, (patch + 1) * per_patch):
                    halo_send(block, 1, part).wait_recv()

            near_pair(block, far_slot, patch, 1)
        for i in range(1, 4):
            wait_weight(block, i)
        if block < last:
            for patch in range(patches):
                attend(patch)
                start_row = patch * patch_rows
                total = feed_forward(block, start_row, patch_rows)
                state[pl.ds(start_row, patch_rows), :] = total
                normed[block + 1, 1, pl.ds(start_row, patch_rows), :] = normalize(total)
                for part in range(patch * per_patch, (patch + 1) * per_patch):
                    halo_send(block + 1, 0, part).start()
        else:
            for patch in range(patches):
                attend(patch)
            state[...] = feed_forward(block, 0, rows)

    row = lax.broadcasted_iota(jnp.int32, (rows, 1), 0)
    kept = jnp.where(row < counts_ref[section, region], state[...], 0.0)
    out_ref[0] = kept
    for block in range(segments):
        for part in range(HALO_PARTS):
            halo_send(block, 0, part).wait_send()

        @pl.when(has_target)
        def _():
            for part in range(HALO_PARTS):
                halo_send(block, 1, part).wait_send()

    for send in weight_sends():
        send.wait_send()


def per_device(hits, order, links, counts, w_qkv, w_out, w_up, w_down):
    segments = lax.axis_size("section")
    regions = lax.axis_size("region")
    rows, width = hits.shape[1:]
    patches = links.shape[1]
    patch_rows = rows // patches
    near_patches = patches + 2 * REACH
    group = LANES * HEADS // width
    assert patches == REACH and regions % 2 == 0 and w_qkv.shape[0] == 1
    piece_count = 4
    vmem = pl.BlockSpec(memory_space=pltpu.VMEM)
    hbm = pl.BlockSpec(memory_space=pltpu.HBM)
    bf16 = jnp.bfloat16
    encoded = pl.pallas_call(
        functools.partial(kernel, segments, regions),
        out_shape=jax.ShapeDtypeStruct((1, rows, width), jnp.float32),
        in_specs=[hbm] * 8,
        out_specs=vmem,
        scratch_shapes=[
            pltpu.VMEM((segments,) + w_qkv.shape[1:], bf16),
            pltpu.VMEM((segments,) + w_out.shape[1:], bf16),
            pltpu.VMEM((segments,) + w_up.shape[1:], bf16),
            pltpu.VMEM((segments,) + w_down.shape[1:], bf16),
            pltpu.VMEM((rows, width), jnp.float32),
            pltpu.VMEM((segments, 3, rows, width), bf16),
            pltpu.VMEM((rows, width), bf16),
            pltpu.VMEM((near_patches, patch_rows, width), bf16),
            pltpu.VMEM((near_patches, patch_rows, width), bf16),
            pltpu.VMEM((rows, width), bf16),
            pltpu.VMEM((patches * (width // LANES), group * patch_rows, 2 * LANES), jnp.float32),
            pltpu.VMEM((patches * (width // LANES), group * patch_rows, 1), jnp.float32),
            pltpu.VMEM((rows, width), bf16),
            pltpu.VMEM(order.shape[1:], jnp.int32),
            pltpu.SMEM(links.shape, jnp.int32),
            pltpu.SMEM(counts.shape, jnp.int32),
            pltpu.SemaphoreType.DMA((4,)),
            pltpu.SemaphoreType.DMA((segments, piece_count)),
            pltpu.SemaphoreType.DMA((segments - 1, piece_count)),
            pltpu.SemaphoreType.DMA((segments, 2, HALO_PARTS)),
            pltpu.SemaphoreType.DMA((segments, 2, HALO_PARTS)),
        ],
        compiler_params=pltpu.CompilerParams(
            collective_id=0, has_side_effects=True, vmem_limit_bytes=60 * 2**20
        ),
        name="blocks",
    )(links, counts, hits, order, w_qkv, w_out, w_up, w_down)
    return encoded.astype(bf16)


def solution(mesh):
    in_specs = (
        P("section", "region", None),
        P(None, "region", None),
        P(None, "region", None),
        P(),
        P("section", None, None),
        P("section", None, None),
        P("section", None, None),
        P("section", None, None),
    )
    out_specs = P("section", "region", None)
    return jax.shard_map(
        per_device, mesh=mesh, in_specs=in_specs, out_specs=out_specs, check_vma=False
    )
```
